32 devices in a mesh: parts: 2 (over y), rep: 4 (over x, core), tp: 4 (over z).
Axes of the slice: x: 2, y: 2, z: 4, core: 2. Of those that a mesh axis runs over, the one named last changes fastest.
Arguments:
- tokens: bfloat16 [8192, 5120], P(('parts', 'rep', 'tp')), parts along dimension 0, may hold values from -6 to 6
- q_weight: bfloat16 [5120, 8192], P(None, 'tp'), may hold values from -0.078125 to 0.078125
- a_store: bfloat16 [1024, 5120, 32], P(('parts', 'rep'), 'tp'), parts along dimension 0, may hold values from -0.078125 to 0.078125
- b_store: bfloat16 [1024, 32, 8192], P(('parts', 'rep'), None, 'tp'), parts along dimension 0, may hold values from -1 to 1
- store_row: int32 [1024], P('parts'), parts along dimension 0, may hold values from 0 to 511, as said below
- block_adapter: int32 [8, 8], P('parts'), parts along dimension 0, may hold values from 0 to 511, as said below
- block_length: int32 [8, 8], P('parts'), parts along dimension 0, may hold values from 1 to 128, as said below
Outputs:
- queries: bfloat16 [8192, 8192], P(('parts', 'rep'), 'tp'), parts along dimension 0
The draws below stay inside these ranges and needn't reach their ends.
There are 2 independent parts, one for each index of `parts`. The reference program is written for one: setup_inputs(seed, part) draws one part's arguments, and reference() takes and returns one part's arrays. A program takes and returns all parts, laid end to end along the dimension named above; an argument that names none is the same for every part. Nothing has to cross between parts.
Inputs may be any that keep to these rules, and one draw needn't show every extreme that they name: `store_row`: a permutation of 0 to 511. `block_adapter`: within one replica's 8 blocks, at most 2 blocks name adapters held by the same replica, and in every replica some holder serves exactly 2 of them. `block_length`: every replica has a block with all 128 rows live.
All inputs are finite; a program needn't handle non-finite values.
Results may differ from the reference program's by a relative error of at most 0.004.
Values may be sent and summed in bfloat16 or wider, within the bound.
A program may use at most 192 MiB of HBM per device.

```python
import jax
import jax.numpy as jnp
from jax import lax

D = 5120
QOUT = 8192
RANK = 32
ADAPTERS = 512
BLOCK_ROWS = 128
TOK_REP = 1024
BLOCKS = 8
SLOTS = 128
TOKENS = 4096
N_REP = 4


def common_order(key):
    return jax.random.permutation(key, ADAPTERS).astype(jnp.int32)


def draw_store_row(key, part):
    return common_order(key)


def draw_block_adapter(key, part):
    placement = common_order(key)
    inverse = jnp.argsort(placement).astype(jnp.int32)
    key = jax.random.fold_in(key, 11)
    keys = jax.random.split(key, 4)
    capacity = max(2, (BLOCKS + N_REP - 1) // N_REP)
    lowest = max(1, -(-(BLOCKS - N_REP) // (capacity - 1)))
    highest = BLOCKS // capacity
    pairs = jax.random.randint(keys[0], (N_REP, 1), lowest, highest + 1).astype(jnp.int32)
    position = jnp.arange(BLOCKS, dtype=jnp.int32)[None, :]
    group = jnp.where(position < capacity * pairs, position // capacity, pairs + position - capacity * pairs)
    owner_order = jax.vmap(lambda sub: jax.random.permutation(sub, N_REP))(jax.random.split(keys[1], N_REP)).astype(jnp.int32)
    owners = jnp.take_along_axis(owner_order, group, axis=1)
    shuffle = jax.vmap(lambda sub: jax.random.permutation(sub, BLOCKS))(jax.random.split(keys[2], N_REP)).astype(jnp.int32)
    owners = jnp.take_along_axis(owners, shuffle, axis=1)
    slot_drawn = jax.random.randint(keys[3], (N_REP, BLOCKS), 0, SLOTS).astype(jnp.int32)
    return jnp.take(inverse, owners * SLOTS + slot_drawn, axis=0)


def draw_block_length(key, part):
    key = jax.random.fold_in(key, 23)
    keys = jax.random.split(key, 2)
    drawn = jax.random.randint(keys[0], (N_REP, BLOCKS), 1, BLOCK_ROWS + 1).astype(jnp.int32)
    full_block = jax.random.randint(keys[1], (N_REP, 1), 0, BLOCKS).astype(jnp.int32)
    position = jnp.arange(BLOCKS, dtype=jnp.int32)[None, :]
    return jnp.where(position == full_block, BLOCK_ROWS, drawn).astype(jnp.int32)


def steps_of(stream_key, extent, pieces, least, top_value):
    def one(axis_at, parts):
        heights = jax.random.uniform(jax.random.fold_in(jax.random.fold_in(stream_key, 6), axis_at), (parts,), jnp.float32, least / len(pieces), top_value / len(pieces))
        return jnp.repeat(jnp.exp(heights), extent[axis_at] // parts).reshape((-1,) + (1,) * (len(extent) - axis_at - 1))

    gain = one(*pieces[0])
    for cut in pieces[1:]:
        gain = gain * one(*cut)
    return gain


def noise(own_key, extent, deviation, most, cuts=(), kind=jnp.bfloat16):
    array = deviation * jax.random.normal(own_key, extent, jnp.float32)
    if cuts:
        array = array * steps_of(own_key, extent, cuts, -0.22, 0.18)
    return jnp.clip(array, -most, most).astype(kind)


def setup_inputs(seed: int = 0, part: int = 0) -> dict:
    splits = jax.random.split(jax.random.key(seed), 8)
    part_keys = jax.random.split(jax.random.fold_in(splits[7], part), 8)
    return {
        "tokens": noise(part_keys[0], (TOKENS, D), 1.0, 6.0, ((0, 16),)),
        "q_weight": noise(splits[1], (D, QOUT), D ** -0.5, 0.078125, ((1, 4),)),
        "a_store": noise(part_keys[2], (ADAPTERS, D, RANK), D ** -0.5, 0.078125, ((0, 4), (1, 4))),
        "b_store": noise(part_keys[3], (ADAPTERS, RANK, QOUT), RANK ** -0.5, 1.0, ((0, 4), (2, 4))),
        "store_row": draw_store_row(jax.random.fold_in(jax.random.fold_in(splits[7], part), 71), part),
        "block_adapter": draw_block_adapter(jax.random.fold_in(jax.random.fold_in(splits[7], part), 71), part),
        "block_length": draw_block_length(jax.random.fold_in(jax.random.fold_in(splits[7], part), 71), part),
    }


def reference(tokens, q_weight, a_store, b_store, store_row, block_adapter, block_length):
    def per_replica(replica):
        rows_in = lax.dynamic_slice_in_dim(tokens, replica * TOK_REP, TOK_REP, 0)
        base_out = jnp.dot(rows_in, q_weight, preferred_element_type=jnp.float32)
        adapter_ids = block_adapter[replica]
        store_rows = jnp.take(store_row, adapter_ids, axis=0)
        shrink_maps = jnp.take(a_store, store_rows, axis=0).astype(jnp.float32)
        expand_maps = jnp.take(b_store, store_rows, axis=0).astype(jnp.float32)
        block_in = rows_in.reshape(BLOCKS, BLOCK_ROWS, D).astype(jnp.float32)
        low_rank = jnp.einsum("bnd,bdr->bnr", block_in, shrink_maps).astype(jnp.bfloat16)
        adapter_out = jnp.einsum("bnr,brq->bnq", low_rank.astype(jnp.float32), expand_maps)
        valid_rows = jnp.arange(BLOCK_ROWS, dtype=jnp.int32)[None, :] < block_length[replica][:, None]
        adapter_out = jnp.where(valid_rows[:, :, None], adapter_out, jnp.float32(0.0))
        return (base_out + adapter_out.reshape(TOK_REP, QOUT)).astype(jnp.bfloat16)

    stacked = lax.map(per_replica, jnp.arange(N_REP, dtype=jnp.int32))
    return stacked.reshape(TOKENS, QOUT)
```

```python
import functools

import jax
import jax.numpy as jnp
from jax import lax
from jax.experimental import pallas as pl
from jax.experimental.pallas import tpu as pltpu
from jax.sharding import PartitionSpec as P

MESH = pl.DeviceIdType.MESH


def kernel(
    n, reps, ch, block_rows,
    recv_ref, live_ref, tok_hbm, w_hbm, a_out, b_out, o_hbm,
    w, toks, obuf, a_in, b_in, a_sel, a_own, low,
    w_sem, own_sem, out_sem, rsend, lsend, trecv,
    a_send, a_recv, b_send, b_recv, ta_send, ta_recv, low_send, low_recv,
):
    me = lax.axis_index("tp")
    rep = lax.axis_index("rep")
    rows_own = toks.shape[1]
    chunks = rows_own // ch
    cols = obuf.shape[1]
    blocks, rank, width = a_sel.shape
    per_dev = a_own.shape[1]
    cap = a_out.shape[1]
    tile = min(512, cols)

    barrier = pltpu.get_barrier_semaphore()
    for i in range(1, n):
        pl.semaphore_signal(
            barrier, inc=1, device_id={"tp": lax.rem(me + i, n)}, device_id_type=MESH)
    for i in range(1, reps):
        pl.semaphore_signal(
            barrier, inc=1, device_id={"rep": lax.rem(rep + i, reps)}, device_id_type=MESH)
    pl.semaphore_wait(barrier, n - 1 + reps - 1)

    def chunk_rows(c):
        return pl.ds(pl.multiple_of(c * ch, ch), ch)

    def send(src, s, c, to, sems):
        return pltpu.make_async_remote_copy(
            src_ref=src, dst_ref=toks.at[s, chunk_rows(c)],
            send_sem=sems.at[s, c], recv_sem=trecv.at[s, c],
            device_id={"tp": to}, device_id_type=MESH)

    def right_send(src, s, c):
        return send(src, s, c, jnp.minimum(me + 1, n - 1), rsend)

    def left_send(src, s, c):
        return send(src, s, c, jnp.maximum(me - 1, 0), lsend)

    def send_own(c):
        src = tok_hbm.at[chunk_rows(c)]

        @pl.when(me < n - 1)
        def _():
            right_send(src, me, c).start()

        @pl.when(me > 0)
        def _():
            left_send(src, me, c).start()

    def rep_copy(src, dst, to, sends, recvs):
        return pltpu.make_async_remote_copy(
            src_ref=src.at[to], dst_ref=dst.at[rep],
            send_sem=sends.at[to], recv_sem=recvs.at[rep],
            device_id={"rep": to}, device_id_type=MESH)

    def rep_arrival(dst, frm, sends, recvs):
        return pltpu.make_async_remote_copy(
            src_ref=dst.at[frm], dst_ref=dst.at[frm],
            send_sem=sends.at[frm], recv_sem=recvs.at[frm],
            device_id={"rep": frm}, device_id_type=MESH)

    early = max(1, chunks // 2)
    for i in range(1, reps):
        rep_copy(a_out, a_in, lax.rem(rep + i, reps), a_send, a_recv).start()
    for c in range(early):
        send_own(c)
    own_a = pltpu.make_async_copy(a_out.at[rep], a_in.at[rep], a_recv.at[rep])
    own_b = pltpu.make_async_copy(b_out.at[rep], b_in.at[rep], b_recv.at[rep])
    own_a.start()
    for i in range(1, reps):
        rep_copy(b_out, b_in, lax.rem(rep + i, reps), b_send, b_recv).start()
    own_b.start()
    own_t = pltpu.make_async_copy(tok_hbm, toks.at[me], own_sem)
    own_t.start()
    w_copy = pltpu.make_async_copy(w_hbm, w, w_sem)
    w_copy.start()

    own_a.wait()
    for i in range(1, reps):
        rep_arrival(a_in, lax.rem(rep + i, reps), a_send, a_recv).wait_recv()
    for b in range(blocks):
        at = recv_ref[b]
        a_sel[b] = a_in[at // cap, at % cap]

    def first_block(d):
        return d * rows_own // block_rows

    def ta_copy(d):
        return pltpu.make_async_remote_copy(
            src_ref=a_sel.at[pl.ds(first_block(d), per_dev)], dst_ref=a_own.at[me],
            send_sem=ta_send.at[d], recv_sem=ta_recv.at[me],
            device_id={"tp": d}, device_id_type=MESH)

    def ta_arrival(d):
        return pltpu.make_async_remote_copy(
            src_ref=a_own.at[d], dst_ref=a_own.at[d],
            send_sem=ta_send.at[d], recv_sem=ta_recv.at[d],
            device_id={"tp": d}, device_id_type=MESH)

    for i in range(1, n):
        ta_copy(lax.rem(me + i, n)).start()
    for c in range(early, chunks):
        send_own(c)
    a_own[me] = a_sel[pl.ds(first_block(me), per_dev)]
    own_t.wait()
    for i in range(1, n):
        ta_arrival(lax.rem(me + i, n)).wait_recv()

    part = rows_own // per_dev
    for j in range(per_dev):
        total = jnp.zeros((part, rank), jnp.float32)
        for k in range(n):
            total += lax.dot_general(
                toks[me, j * part:(j + 1) * part, k * width:(k + 1) * width], a_own[k, j],
                (((1,), (1,)), ((), ())), preferred_element_type=jnp.float32)
        low[me, j * part:(j + 1) * part, :] = total.astype(jnp.bfloat16)

    def low_copy(d):
        return pltpu.make_async_remote_copy(
            src_ref=low.at[me], dst_ref=low.at[me],
            send_sem=low_send.at[d], recv_sem=low_recv.at[me],
            device_id={"tp": d}, device_id_type=MESH)

    def low_arrival(d):
        return pltpu.make_async_remote_copy(
            src_ref=low.at[d], dst_ref=low.at[d],
            send_sem=low_send.at[d], recv_sem=low_recv.at[d],
            device_id={"tp": d}, device_id_type=MESH)

    for i in range(1, n):
        low_copy(lax.rem(me + i, n)).start()

    own_b.wait()
    for i in range(1, reps):
        rep_arrival(b_in, lax.rem(rep + i, reps), b_send, b_recv).wait_recv()
    w_copy.wait()

    def out_copy(s, c):
        at = pl.ds(pl.multiple_of(s * rows_own + c * ch, ch), ch)
        return pltpu.make_async_copy(obuf.at[at], o_hbm.at[at], out_sem.at[s, c])

    def multiply(s, c):
        block = (s * rows_own + c * ch) // block_rows
        inside = lax.rem(s * rows_own + c * ch, block_rows)
        at = recv_ref[block]
        live = live_ref[block]
        here = pl.ds(pl.multiple_of(s * rows_own + c * ch, ch), ch)
        valid = inside + lax.broadcasted_iota(jnp.int32, (ch, tile), 0) < live

        @pl.loop(0, cols // tile)
        def _(t):
            cs = pl.ds(pl.multiple_of(t * tile, tile), tile)
            extra = jnp.dot(
                low[s, chunk_rows(c), :], b_in[at // cap, at % cap, :, cs],
                preferred_element_type=jnp.float32)
            base = jnp.dot(
                toks[s, chunk_rows(c), :], w[:, cs], preferred_element_type=jnp.float32)
            obuf[here, cs] = (base + jnp.where(valid, extra, 0.0)).astype(jnp.bfloat16)

        out_copy(s, c).start()

    @pl.loop(0, chunks)
    def _(c):
        multiply(me, c)

    @pl.loop(0, (n - 1) * chunks)
    def _(e):
        k = e // chunks + 1
        c = lax.rem(e, chunks)
        from_left = jnp.maximum(me - k, 0)
        from_right = jnp.minimum(me + k, n - 1)

        @pl.when(me - k >= 0)
        def _():
            here = toks.at[from_left, chunk_rows(c)]
            right_send(here, from_left, c).wait_recv()

            @pl.when(me < n - 1)
            def _():
                right_send(here, from_left, c).start()

        @pl.when(me + k < n)
        def _():
            here = toks.at[from_right, chunk_rows(c)]
            left_send(here, from_right, c).wait_recv()

            @pl.when(me > 0)
            def _():
                left_send(here, from_right, c).start()

        @pl.when(me - k >= 0)
        def _():
            @pl.when(c == 0)
            def _():
                low_arrival(from_left).wait_recv()

            multiply(from_left, c)

        @pl.when(me + k < n)
        def _():
            @pl.when(c == 0)
            def _():
                low_arrival(from_right).wait_recv()

            multiply(from_right, c)

    for i in range(1, reps):
        to = lax.rem(rep + i, reps)
        rep_copy(a_out, a_in, to, a_send, a_recv).wait_send()
        rep_copy(b_out, b_in, to, b_send, b_recv).wait_send()
    for i in range(1, n):
        to = lax.rem(me + i, n)
        ta_copy(to).wait_send()
        low_copy(to).wait_send()

    @pl.loop(0, n * chunks)
    def _(e):
        s = e // chunks
        c = lax.rem(e, chunks)
        here = toks.at[s, chunk_rows(c)]
        out_copy(s, c).wait()

        @pl.when((s <= me) & (me < n - 1))
        def _():
            right_send(here, s, c).wait_send()

        @pl.when((s >= me) & (me > 0))
        def _():
            left_send(here, s, c).wait_send()


def per_device(tokens, q_weight, a_store, b_store, store_row, block_adapter, block_length):
    n = lax.axis_size("tp")
    reps = lax.axis_size("rep")
    here_rep = lax.axis_index("rep")
    slot_count, width, rank = a_store.shape
    cols = b_store.shape[2]
    rows_own, model_width = tokens.shape
    blocks = block_adapter.shape[1]
    cap = max(2, -(-blocks // reps))
    block_rows = rows_own * n // blocks
    ch = min(64, rows_own)
    chunks = rows_own // ch
    per_dev = max(1, rows_own // block_rows)

    stored = jnp.take(store_row, block_adapter, axis=0, mode="clip")
    owner = stored // slot_count
    slot = stored % slot_count
    ids = jnp.arange(blocks, dtype=jnp.int32)
    earlier = (owner[:, :, None] == owner[:, None, :]) & (ids[None, None, :] < ids[None, :, None])
    place = jnp.sum(earlier.astype(jnp.int32), axis=2)
    picked = (owner == here_rep)[:, None, :] & (
        place[:, None, :] == jnp.arange(cap, dtype=jnp.int32)[None, :, None])
    source = jnp.sum(jnp.where(picked, slot[:, None, :], 0), axis=2).reshape(-1)
    a_t = jnp.transpose(a_store, (0, 2, 1))
    a_out = jnp.take(a_t, source, axis=0, mode="clip").reshape(reps, cap, rank, width)
    b_out = jnp.take(b_store, source, axis=0, mode="clip").reshape(reps, cap, rank, cols)
    mine = (jnp.arange(reps, dtype=jnp.int32) == here_rep)[:, None]
    recv = jnp.sum(jnp.where(mine, owner * cap + place, 0), axis=0)
    live = jnp.sum(jnp.where(mine, block_length, 0), axis=0)

    any_spec = pl.BlockSpec(memory_space=pl.ANY)
    smem = pl.BlockSpec(memory_space=pltpu.SMEM)
    dma = pltpu.SemaphoreType.DMA
    bf16 = jnp.bfloat16
    rows = rows_own * n
    return pl.pallas_call(
        functools.partial(kernel, n, reps, ch, block_rows),
        out_shape=jax.ShapeDtypeStruct((rows, cols), bf16),
        in_specs=[smem, smem, any_spec, any_spec, any_spec, any_spec],
        out_specs=any_spec,
        scratch_shapes=[
            pltpu.VMEM((model_width, cols), bf16),
            pltpu.VMEM((n, rows_own, model_width), bf16),
            pltpu.VMEM((rows, cols), bf16),
            pltpu.VMEM((reps, cap, rank, width), bf16),
            pltpu.VMEM((reps, cap, rank, cols), bf16),
            pltpu.VMEM((blocks, rank, width), bf16),
            pltpu.VMEM((n, per_dev, rank, width), bf16),
            pltpu.VMEM((n, rows_own, rank), bf16),
            dma, dma, dma((n, chunks)), dma((n, chunks)), dma((n, chunks)), dma((n, chunks)),
            dma((reps,)), dma((reps,)), dma((reps,)), dma((reps,)),
            dma((n,)), dma((n,)), dma((n,)), dma((n,)),
        ],
        compiler_params=pltpu.CompilerParams(
            collective_id=0, has_side_effects=True, vmem_limit_bytes=50 * 1024 * 1024),
        cost_estimate=pl.CostEstimate(
            flops=2 * rows * model_width * cols, bytes_accessed=2 * model_width * cols,
            transcendentals=0),
    )(recv, live, tokens, q_weight, a_out, b_out)


def solution(mesh):
    return jax.shard_map(
        per_device,
        mesh=mesh,
        in_specs=(
            P(("parts", "rep", "tp"), None),
            P(None, "tp"),
            P(("parts", "rep"), "tp", None),
            P(("parts", "rep"), None, "tp"),
            P("parts"),
            P("parts", None),
            P("parts", None),
        ),
        out_specs=P(("parts", "rep"), "tp"),
        check_vma=False,
    )
```

```python
import functools

import jax
import jax.numpy as jnp
from jax import lax
from jax.experimental import pallas as pl
from jax.experimental.pallas import tpu as pltpu
from jax.sharding import PartitionSpec as P

MESH = pl.DeviceIdType.MESH


def kernel(
    n, reps, ch, block_rows,
    recv_ref, live_ref, tok_hbm, w_hbm, a_out, b_out, o_hbm,
    w, toks, obuf, a_in, b_in, a_sel, a_own, low, low_t,
    w_sem, own_sem, out_sem, rsend, lsend, trecv,
    a_send, a_recv, b_send, b_recv, ta_send, ta_recv, low_send, low_recv,
):
    me = lax.axis_index("tp")
    rep = lax.axis_index("rep")
    rows_own = toks.shape[1]
    chunks = rows_own // ch
    cols = obuf.shape[1]
    blocks, rank, width = a_sel.shape
    per_dev = a_own.shape[1]
    cap = a_out.shape[1]
    tile = min(512, cols)

    barrier = pltpu.get_barrier_semaphore()
    for i in range(1, n):
        pl.semaphore_signal(
            barrier, inc=1, device_id={"tp": lax.rem(me + i, n)}, device_id_type=MESH)
    for i in range(1, reps):
        pl.semaphore_signal(
            barrier, inc=1, device_id={"rep": lax.rem(rep + i, reps)}, device_id_type=MESH)
    pl.semaphore_wait(barrier, n - 1 + reps - 1)

    def chunk_rows(c):
        return pl.ds(pl.multiple_of(c * ch, ch), ch)

    def send(src, s, c, to, sems):
        return pltpu.make_async_remote_copy(
            src_ref=src, dst_ref=toks.at[s, chunk_rows(c)],
            send_sem=sems.at[s, c], recv_sem=trecv.at[s, c],
            device_id={"tp": to}, device_id_type=MESH)

    def right_send(src, s, c):
        return send(src, s, c, jnp.minimum(me + 1, n - 1), rsend)

    def left_send(src, s, c):
        return send(src, s, c, jnp.maximum(me - 1, 0), lsend)

    def send_own(c):
        src = tok_hbm.at[chunk_rows(c)]

        @pl.when(me < n - 1)
        def _():
            right_send(src, me, c).start()

        @pl.when(me > 0)
        def _():
            left_send(src, me, c).start()

    def rep_copy(src, dst, to, sends, recvs):
        return pltpu.make_async_remote_copy(
            src_ref=src.at[to], dst_ref=dst.at[rep],
            send_sem=sends.at[to], recv_sem=recvs.at[rep],
            device_id={"rep": to}, device_id_type=MESH)

    def rep_arrival(dst, frm, sends, recvs):
        return pltpu.make_async_remote_copy(
            src_ref=dst.at[frm], dst_ref=dst.at[frm],
            send_sem=sends.at[frm], recv_sem=recvs.at[frm],
            device_id={"rep": frm}, device_id_type=MESH)

    early = max(1, chunks // 2)
    for i in range(1, reps):
        rep_copy(a_out, a_in, lax.rem(rep + i, reps), a_send, a_recv).start()
    for c in range(early):
        send_own(c)
    own_a = pltpu.make_async_copy(a_out.at[rep], a_in.at[rep], a_recv.at[rep])
    own_b = pltpu.make_async_copy(b_out.at[rep], b_in.at[rep], b_recv.at[rep])
    own_a.start()
    for i in range(1, reps):
        rep_copy(b_out, b_in, lax.rem(rep + i, reps), b_send, b_recv).start()
    own_b.start()
    own_t = pltpu.make_async_copy(tok_hbm, toks.at[me], own_sem)
    own_t.start()
    w_copy = pltpu.make_async_copy(w_hbm, w, w_sem)
    w_copy.start()

    own_a.wait()
    for i in range(1, reps):
        rep_arrival(a_in, lax.rem(rep + i, reps), a_send, a_recv).wait_recv()
    for b in range(blocks):
        at = recv_ref[b]
        a_sel[b] = a_in[at // cap, at % cap]

    def first_block(d):
        return d * rows_own // block_rows

    def ta_copy(d):
        return pltpu.make_async_remote_copy(
            src_ref=a_sel.at[pl.ds(first_block(d), per_dev)], dst_ref=a_own.at[me],
            send_sem=ta_send.at[d], recv_sem=ta_recv.at[me],
            device_id={"tp": d}, device_id_type=MESH)

    def ta_arrival(d):
        return pltpu.make_async_remote_copy(
            src_ref=a_own.at[d], dst_ref=a_own.at[d],
            send_sem=ta_send.at[d], recv_sem=ta_recv.at[d],
            device_id={"tp": d}, device_id_type=MESH)

    for i in range(1, n):
        ta_copy(lax.rem(me + i, n)).start()
    for c in range(early, chunks):
        send_own(c)
    a_own[me] = a_sel[pl.ds(first_block(me), per_dev)]
    own_t.wait()
    for i in range(1, n):
        ta_arrival(lax.rem(me + i, n)).wait_recv()

    part = rows_own // per_dev
    for j in range(per_dev):
        total = jnp.zeros((part, rank), jnp.float32)
        for k in range(n):
            total += lax.dot_general(
                toks[me, j * part:(j + 1) * part, k * width:(k + 1) * width], a_own[k, j],
                (((1,), (1,)), ((), ())), preferred_element_type=jnp.float32)
        low[me, j * part:(j + 1) * part, :] = total.astype(jnp.bfloat16)
        low_t[me, :, j * part:(j + 1) * part] = total.T.astype(jnp.bfloat16)

    def low_copy(d):
        return pltpu.make_async_remote_copy(
            src_ref=low_t.at[me], dst_ref=low_t.at[me],
            send_sem=low_send.at[d], recv_sem=low_recv.at[me],
            device_id={"tp": d}, device_id_type=MESH)

    def low_arrival(d):
        return pltpu.make_async_remote_copy(
            src_ref=low_t.at[d], dst_ref=low_t.at[d],
            send_sem=low_send.at[d], recv_sem=low_recv.at[d],
            device_id={"tp": d}, device_id_type=MESH)

    for i in range(1, n):
        low_copy(lax.rem(me + i, n)).start()

    own_b.wait()
    for i in range(1, reps):
        rep_arrival(b_in, lax.rem(rep + i, reps), b_send, b_recv).wait_recv()
    w_copy.wait()

    def out_copy(s, c):
        at = pl.ds(pl.multiple_of(s * rows_own + c * ch, ch), ch)
        return pltpu.make_async_copy(obuf.at[at], o_hbm.at[at], out_sem.at[s, c])

    def multiply(s, c):
        block = (s * rows_own + c * ch) // block_rows
        inside = lax.rem(s * rows_own + c * ch, block_rows)
        at = recv_ref[block]
        live = live_ref[block]
        here = pl.ds(pl.multiple_of(s * rows_own + c * ch, ch), ch)
        valid = inside + lax.broadcasted_iota(jnp.int32, (ch, tile), 0) < live

        @pl.loop(0, cols // tile)
        def _(t):
            cs = pl.ds(pl.multiple_of(t * tile, tile), tile)
            extra = jnp.dot(
                low[s, chunk_rows(c), :], b_in[at // cap, at % cap, :, cs],
                preferred_element_type=jnp.float32)
            base = jnp.dot(
                toks[s, chunk_rows(c), :], w[:, cs], preferred_element_type=jnp.float32)
            obuf[here, cs] = (base + jnp.where(valid, extra, 0.0)).astype(jnp.bfloat16)

        out_copy(s, c).start()

    def take_low(s):
        low_arrival(s).wait_recv()
        low[s] = low_t[s].astype(jnp.float32).T.astype(jnp.bfloat16)

    @pl.loop(0, (n - 1) * chunks)
    def _(e):
        k = e // chunks + 1
        c = lax.rem(e, chunks)
        from_left = jnp.maximum(me - k, 0)
        from_right = jnp.minimum(me + k, n - 1)

        @pl.when(me - k >= 0)
        def _():
            here = toks.at[from_left, chunk_rows(c)]
            right_send(here, from_left, c).wait_recv()

            @pl.when(me < n - 1)
            def _():
                right_send(here, from_left, c).start()

        @pl.when(me + k < n)
        def _():
            here = toks.at[from_right, chunk_rows(c)]
            left_send(here, from_right, c).wait_recv()

            @pl.when(me > 0)
            def _():
                left_send(here, from_right, c).start()

        @pl.when(me - k >= 0)
        def _():
            @pl.when(c == 0)
            def _():
                take_low(from_left)

            multiply(from_left, c)

        @pl.when(me + k < n)
        def _():
            @pl.when(c == 0)
            def _():
                take_low(from_right)

            multiply(from_right, c)

        @pl.when(k == min(2, n - 1))
        def _():
            multiply(me, c)

    for i in range(1, reps):
        to = lax.rem(rep + i, reps)
        rep_copy(a_out, a_in, to, a_send, a_recv).wait_send()
        rep_copy(b_out, b_in, to, b_send, b_recv).wait_send()
    for i in range(1, n):
        to = lax.rem(me + i, n)
        ta_copy(to).wait_send()
        low_copy(to).wait_send()

    @pl.loop(0, n * chunks)
    def _(e):
        s = e // chunks
        c = lax.rem(e, chunks)
        here = toks.at[s, chunk_rows(c)]
        out_copy(s, c).wait()

        @pl.when((s <= me) & (me < n - 1))
        def _():
            right_send(here, s, c).wait_send()

        @pl.when((s >= me) & (me > 0))
        def _():
            left_send(here, s, c).wait_send()


def fetch(
    reps, cap,
    row_ref, adapter_ref, length_ref, a_hbm, b_hbm, a_out, b_out, recv_ref, live_ref,
    source, seen, a_sem, b_sem,
):
    rep = lax.axis_index("rep")
    slots = a_hbm.shape[0]
    blocks = adapter_ref.shape[1]
    for i in range(reps * cap):
        source[i] = 0
    for i in range(reps):
        seen[i] = 0

    @pl.loop(0, reps)
    def _(r):
        def block(b, held):
            stored = row_ref[adapter_ref[r, b]]
            mine = stored // slots == rep

            @pl.when(mine)
            def _():
                source[r * cap + jnp.minimum(held, cap - 1)] = stored % slots

            return held + mine.astype(jnp.int32)

        lax.fori_loop(0, blocks, block, jnp.int32(0))

    def copies(i):
        at = source[i]
        return (
            pltpu.make_async_copy(a_hbm.at[at], a_out.at[i], a_sem.at[i]),
            pltpu.make_async_copy(b_hbm.at[at], b_out.at[i], b_sem.at[i]),
        )

    for i in range(reps * cap):
        for copy in copies(i):
            copy.start()

    @pl.loop(0, blocks)
    def _(b):
        owner = row_ref[adapter_ref[rep, b]] // slots
        place = seen[owner]
        recv_ref[b] = owner * cap + place
        seen[owner] = place + 1
        live_ref[b] = length_ref[rep, b]

    for i in range(reps * cap):
        for copy in copies(i):
            copy.wait()


def per_device(tokens, q_weight, a_store, b_store, store_row, block_adapter, block_length):
    n = lax.axis_size("tp")
    reps = lax.axis_size("rep")
    here_rep = lax.axis_index("rep")
    slot_count, width, rank = a_store.shape
    cols = b_store.shape[2]
    rows_own, model_width = tokens.shape
    blocks = block_adapter.shape[1]
    cap = max(2, -(-blocks // reps))
    block_rows = rows_own * n // blocks
    ch = min(64, rows_own)
    chunks = rows_own // ch
    per_dev = max(1, rows_own // block_rows)

    any_spec = pl.BlockSpec(memory_space=pl.ANY)
    smem = pl.BlockSpec(memory_space=pltpu.SMEM)
    dma = pltpu.SemaphoreType.DMA
    bf16 = jnp.bfloat16
    rows = rows_own * n
    a_t = jnp.transpose(a_store, (0, 2, 1))
    a_out, b_out, recv, live = pl.pallas_call(
        functools.partial(fetch, reps, cap),
        out_shape=(
            jax.ShapeDtypeStruct((reps * cap, rank, width), bf16),
            jax.ShapeDtypeStruct((reps * cap, rank, cols), bf16),
            jax.ShapeDtypeStruct((blocks,), jnp.int32),
            jax.ShapeDtypeStruct((blocks,), jnp.int32),
        ),
        in_specs=[smem, smem, smem, any_spec, any_spec],
        out_specs=(any_spec, any_spec, smem, smem),
        scratch_shapes=[
            pltpu.SMEM((reps * cap,), jnp.int32), pltpu.SMEM((reps,), jnp.int32),
            dma((reps * cap,)), dma((reps * cap,)),
        ],
    )(store_row, block_adapter, block_length, a_t, b_store)
    a_out = a_out.reshape(reps, cap, rank, width)
    b_out = b_out.reshape(reps, cap, rank, cols)
    return pl.pallas_call(
        functools.partial(kernel, n, reps, ch, block_rows),
        out_shape=jax.ShapeDtypeStruct((rows, cols), bf16),
        in_specs=[smem, smem, any_spec, any_spec, any_spec, any_spec],
        out_specs=any_spec,
        scratch_shapes=[
            pltpu.VMEM((model_width, cols), bf16),
            pltpu.VMEM((n, rows_own, model_width), bf16),
            pltpu.VMEM((rows, cols), bf16),
            pltpu.VMEM((reps, cap, rank, width), bf16),
            pltpu.VMEM((reps, cap, rank, cols), bf16),
            pltpu.VMEM((blocks, rank, width), bf16),
            pltpu.VMEM((n, per_dev, rank, width), bf16),
            pltpu.VMEM((n, rows_own, rank), bf16),
            pltpu.VMEM((n, rank, rows_own), bf16),
            dma, dma, dma((n, chunks)), dma((n, chunks)), dma((n, chunks)), dma((n, chunks)),
            dma((reps,)), dma((reps,)), dma((reps,)), dma((reps,)),
            dma((n,)), dma((n,)), dma((n,)), dma((n,)),
        ],
        compiler_params=pltpu.CompilerParams(
            collective_id=0, has_side_effects=True, vmem_limit_bytes=44 * 1024 * 1024),
        cost_estimate=pl.CostEstimate(
            flops=2 * rows * model_width * cols, bytes_accessed=2 * model_width * cols,
            transcendentals=0),
    )(recv, live, tokens, q_weight, a_out, b_out)


def solution(mesh):
    return jax.shard_map(
        per_device,
        mesh=mesh,
        in_specs=(
            P(("parts", "rep", "tp"), None),
            P(None, "tp"),
            P(("parts", "rep"), "tp", None),
            P(("parts", "rep"), None, "tp"),
            P("parts"),
            P("parts", None),
            P("parts", None),
        ),
        out_specs=P(("parts", "rep"), "tp"),
        check_vma=False,
    )
```

```python
import functools

import jax
import jax.numpy as jnp
from jax import lax
from jax.experimental import pallas as pl
from jax.experimental.pallas import tpu as pltpu
from jax.sharding import PartitionSpec as P

MESH = pl.DeviceIdType.MESH


def kernel(
    n, reps, depth, block_rows,
    recv_ref, live_ref, tok_hbm, w_hbm, a_out, b_out, o_hbm,
    w, toks, obuf, acc, a_in, b_in, a_sel, a_own, low, low_t,
    w_sem, own_sem, out_sem, rsend, lsend, trecv,
    a_send, a_recv, b_send, b_recv, ta_send, ta_recv, low_send, low_recv,
):
    me = lax.axis_index("tp")
    rep = lax.axis_index("rep")
    rows_own = toks.shape[1]
    chunks = toks.shape[2] // depth
    cols = obuf.shape[1]
    blocks, rank, width = a_sel.shape
    per_dev = a_own.shape[1]
    cap = a_out.shape[1]
    tile = min(512, cols)

    barrier = pltpu.get_barrier_semaphore()
    for i in range(1, n):
        pl.semaphore_signal(
            barrier, inc=1, device_id={"tp": lax.rem(me + i, n)}, device_id_type=MESH)
    for i in range(1, reps):
        pl.semaphore_signal(
            barrier, inc=1, device_id={"rep": lax.rem(rep + i, reps)}, device_id_type=MESH)
    pl.semaphore_wait(barrier, n - 1 + reps - 1)

    def part_of(c):
        return pl.ds(pl.multiple_of(c * depth, depth), depth)

    def send(src, s, c, to, sems):
        return pltpu.make_async_remote_copy(
            src_ref=src, dst_ref=toks.at[s, :, part_of(c)],
            send_sem=sems.at[s, c], recv_sem=trecv.at[s, c],
            device_id={"tp": to}, device_id_type=MESH)

    def right_send(src, s, c):
        return send(src, s, c, jnp.minimum(me + 1, n - 1), rsend)

    def left_send(src, s, c):
        return send(src, s, c, jnp.maximum(me - 1, 0), lsend)

    def send_own(c):
        src = tok_hbm.at[:, part_of(c)]

        @pl.when(me < n - 1)
        def _():
            right_send(src, me, c).start()

        @pl.when(me > 0)
        def _():
            left_send(src, me, c).start()

    def rep_copy(src, dst, to, sends, recvs):
        return pltpu.make_async_remote_copy(
            src_ref=src.at[to], dst_ref=dst.at[rep],
            send_sem=sends.at[to], recv_sem=recvs.at[rep],
            device_id={"rep": to}, device_id_type=MESH)

    def rep_arrival(dst, frm, sends, recvs):
        return pltpu.make_async_remote_copy(
            src_ref=dst.at[frm], dst_ref=dst.at[frm],
            send_sem=sends.at[frm], recv_sem=recvs.at[frm],
            device_id={"rep": frm}, device_id_type=MESH)

    early = max(1, chunks // 2)
    for i in range(1, reps):
        rep_copy(a_out, a_in, lax.rem(rep + i, reps), a_send, a_recv).start()
    for c in range(early):
        send_own(c)
    own_a = pltpu.make_async_copy(a_out.at[rep], a_in.at[rep], a_recv.at[rep])
    own_b = pltpu.make_async_copy(b_out.at[rep], b_in.at[rep], b_recv.at[rep])
    own_a.start()
    for i in range(1, reps):
        rep_copy(b_out, b_in, lax.rem(rep + i, reps), b_send, b_recv).start()
    own_b.start()
    own_t = pltpu.make_async_copy(tok_hbm, toks.at[me], own_sem)
    own_t.start()
    w_copy = pltpu.make_async_copy(w_hbm, w, w_sem)
    w_copy.start()

    own_a.wait()
    for i in range(1, reps):
        rep_arrival(a_in, lax.rem(rep + i, reps), a_send, a_recv).wait_recv()
    for b in range(blocks):
        at = recv_ref[b]
        a_sel[b] = a_in[at // cap, at % cap]

    def first_block(d):
        return d * rows_own // block_rows

    def ta_copy(d):
        return pltpu.make_async_remote_copy(
            src_ref=a_sel.at[pl.ds(first_block(d), per_dev)], dst_ref=a_own.at[me],
            send_sem=ta_send.at[d], recv_sem=ta_recv.at[me],
            device_id={"tp": d}, device_id_type=MESH)

    def ta_arrival(d):
        return pltpu.make_async_remote_copy(
            src_ref=a_own.at[d], dst_ref=a_own.at[d],
            send_sem=ta_send.at[d], recv_sem=ta_recv.at[d],
            device_id={"tp": d}, device_id_type=MESH)

    for i in range(1, n):
        ta_copy(lax.rem(me + i, n)).start()
    for c in range(early, chunks):
        send_own(c)
    a_own[me] = a_sel[pl.ds(first_block(me), per_dev)]
    own_t.wait()
    for i in range(1, n):
        ta_arrival(lax.rem(me + i, n)).wait_recv()

    part = rows_own // per_dev
    for j in range(per_dev):
        total = jnp.zeros((part, rank), jnp.float32)
        for k in range(n):
            total += lax.dot_general(
                toks[me, j * part:(j + 1) * part, k * width:(k + 1) * width], a_own[k, j],
                (((1,), (1,)), ((), ())), preferred_element_type=jnp.float32)
        low[me, j * part:(j + 1) * part, :] = total.astype(jnp.bfloat16)
        low_t[me, :, j * part:(j + 1) * part] = total.T.astype(jnp.bfloat16)

    def low_copy(d):
        return pltpu.make_async_remote_copy(
            src_ref=low_t.at[me], dst_ref=low_t.at[me],
            send_sem=low_send.at[d], recv_sem=low_recv.at[me],
            device_id={"tp": d}, device_id_type=MESH)

    def low_arrival(d):
        return pltpu.make_async_remote_copy(
            src_ref=low_t.at[d], dst_ref=low_t.at[d],
            send_sem=low_send.at[d], recv_sem=low_recv.at[d],
            device_id={"tp": d}, device_id_type=MESH)

    for i in range(1, n):
        low_copy(lax.rem(me + i, n)).start()

    own_b.wait()
    for i in range(1, reps):
        rep_arrival(b_in, lax.rem(rep + i, reps), b_send, b_recv).wait_recv()
    w_copy.wait()

    def out_rows(s):
        return pl.ds(pl.multiple_of(s * rows_own, rows_own), rows_own)

    def out_copy(s):
        return pltpu.make_async_copy(obuf.at[out_rows(s)], o_hbm.at[out_rows(s)], out_sem.at[s])

    def tiles(body):
        @pl.loop(0, cols // tile)
        def _(t):
            body(pl.ds(pl.multiple_of(t * tile, tile), tile))

    def adapter(s, side):
        for j in range(per_dev):
            first = s * rows_own + j * part
            block = first // block_rows
            at = recv_ref[block]
            at_row = lax.broadcasted_iota(jnp.int32, (part, tile), 0)
            valid = lax.rem(first, block_rows) + at_row < live_ref[block]

            def body(cs):
                extra = jnp.dot(
                    low[s, j * part:(j + 1) * part, :], b_in[at // cap, at % cap, :, cs],
                    preferred_element_type=jnp.float32)
                acc[side, j * part:(j + 1) * part, cs] = jnp.where(valid, extra, 0.0)

            tiles(body)

    def multiply(s, c, side):
        @pl.when(c == 0)
        def _():
            adapter(s, side)

        def product(cs):
            return acc[side, :, cs] + jnp.dot(
                toks[s, :, part_of(c)], w[part_of(c), cs], preferred_element_type=jnp.float32)

        @pl.when(c < chunks - 1)
        def _():
            def body(cs):
                acc[side, :, cs] = product(cs)

            tiles(body)

        @pl.when(c == chunks - 1)
        def _():
            def body(cs):
                obuf[out_rows(s), cs] = product(cs).astype(jnp.bfloat16)

            tiles(body)
            out_copy(s).start()

    def take_low(s):
        low_arrival(s).wait_recv()
        low[s] = low_t[s].astype(jnp.float32).T.astype(jnp.bfloat16)

    @pl.loop(0, (n - 1) * chunks)
    def _(e):
        k = e // chunks + 1
        c = lax.rem(e, chunks)
        from_left = jnp.maximum(me - k, 0)
        from_right = jnp.minimum(me + k, n - 1)

        @pl.when(me - k >= 0)
        def _():
            here = toks.at[from_left, :, part_of(c)]
            right_send(here, from_left, c).wait_recv()

            @pl.when(me < n - 1)
            def _():
                right_send(here, from_left, c).start()

        @pl.when(me + k < n)
        def _():
            here = toks.at[from_right, :, part_of(c)]
            left_send(here, from_right, c).wait_recv()

            @pl.when(me > 0)
            def _():
                left_send(here, from_right, c).start()

        @pl.when(me - k >= 0)
        def _():
            @pl.when(c == 0)
            def _():
                take_low(from_left)

            multiply(from_left, c, 0)

        @pl.when(me + k < n)
        def _():
            @pl.when(c == 0)
            def _():
                take_low(from_right)

            multiply(from_right, c, 1)

        @pl.when(k == min(2, n - 1))
        def _():
            multiply(me, c, 2)

    for i in range(1, reps):
        to = lax.rem(rep + i, reps)
        rep_copy(a_out, a_in, to, a_send, a_recv).wait_send()
        rep_copy(b_out, b_in, to, b_send, b_recv).wait_send()
    for i in range(1, n):
        to = lax.rem(me + i, n)
        ta_copy(to).wait_send()
        low_copy(to).wait_send()

    @pl.loop(0, n)
    def _(s):
        out_copy(s).wait()

    @pl.loop(0, n * chunks)
    def _(e):
        s = e // chunks
        c = lax.rem(e, chunks)
        here = toks.at[s, :, part_of(c)]

        @pl.when((s <= me) & (me < n - 1))
        def _():
            right_send(here, s, c).wait_send()

        @pl.when((s >= me) & (me > 0))
        def _():
            left_send(here, s, c).wait_send()


def fetch(
    reps, cap,
    row_ref, adapter_ref, length_ref, a_hbm, b_hbm, a_out, b_out, recv_ref, live_ref,
    source, seen, a_sem, b_sem,
):
    rep = lax.axis_index("rep")
    slots = a_hbm.shape[0]
    blocks = adapter_ref.shape[1]
    for i in range(reps * cap):
        source[i] = 0
    for i in range(reps):
        seen[i] = 0

    @pl.loop(0, reps)
    def _(r):
        def block(b, held):
            stored = row_ref[adapter_ref[r, b]]
            mine = stored // slots == rep

            @pl.when(mine)
            def _():
                source[r * cap + jnp.minimum(held, cap - 1)] = stored % slots

            return held + mine.astype(jnp.int32)

        lax.fori_loop(0, blocks, block, jnp.int32(0))

    def copies(i):
        at = source[i]
        return (
            pltpu.make_async_copy(a_hbm.at[at], a_out.at[i], a_sem.at[i]),
            pltpu.make_async_copy(b_hbm.at[at], b_out.at[i], b_sem.at[i]),
        )

    for i in range(reps * cap):
        for copy in copies(i):
            copy.start()

    @pl.loop(0, blocks)
    def _(b):
        owner = row_ref[adapter_ref[rep, b]] // slots
        place = seen[owner]
        recv_ref[b] = owner * cap + place
        seen[owner] = place + 1
        live_ref[b] = length_ref[rep, b]

    for i in range(reps * cap):
        for copy in copies(i):
            copy.wait()


def per_device(tokens, q_weight, a_store, b_store, store_row, block_adapter, block_length):
    n = lax.axis_size("tp")
    reps = lax.axis_size("rep")
    here_rep = lax.axis_index("rep")
    slot_count, width, rank = a_store.shape
    cols = b_store.shape[2]
    rows_own, model_width = tokens.shape
    blocks = block_adapter.shape[1]
    cap = max(2, -(-blocks // reps))
    block_rows = rows_own * n // blocks
    depth = model_width // 5
    chunks = model_width // depth
    per_dev = max(1, rows_own // block_rows)

    any_spec = pl.BlockSpec(memory_space=pl.ANY)
    smem = pl.BlockSpec(memory_space=pltpu.SMEM)
    vmem = pl.BlockSpec(memory_space=pltpu.VMEM)
    dma = pltpu.SemaphoreType.DMA
    bf16 = jnp.bfloat16
    rows = rows_own * n
    a_t = jnp.transpose(a_store, (0, 2, 1))
    a_out, b_out, recv, live = pl.pallas_call(
        functools.partial(fetch, reps, cap),
        out_shape=(
            jax.ShapeDtypeStruct((reps * cap, rank, width), bf16),
            jax.ShapeDtypeStruct((reps * cap, rank, cols), bf16),
            jax.ShapeDtypeStruct((blocks,), jnp.int32),
            jax.ShapeDtypeStruct((blocks,), jnp.int32),
        ),
        in_specs=[smem, smem, smem, any_spec, any_spec],
        out_specs=(vmem, vmem, smem, smem),
        scratch_shapes=[
            pltpu.SMEM((reps * cap,), jnp.int32), pltpu.SMEM((reps,), jnp.int32),
            dma((reps * cap,)), dma((reps * cap,)),
        ],
    )(store_row, block_adapter, block_length, a_t, b_store)
    a_out = a_out.reshape(reps, cap, rank, width)
    b_out = b_out.reshape(reps, cap, rank, cols)
    return pl.pallas_call(
        functools.partial(kernel, n, reps, depth, block_rows),
        out_shape=jax.ShapeDtypeStruct((rows, cols), bf16),
        in_specs=[smem, smem, any_spec, any_spec, any_spec, any_spec],
        out_specs=any_spec,
        scratch_shapes=[
            pltpu.VMEM((model_width, cols), bf16),
            pltpu.VMEM((n, rows_own, model_width), bf16),
            pltpu.VMEM((rows, cols), bf16),
            pltpu.VMEM((3, rows_own, cols), jnp.float32),
            pltpu.VMEM((reps, cap, rank, width), bf16),
            pltpu.VMEM((reps, cap, rank, cols), bf16),
            pltpu.VMEM((blocks, rank, width), bf16),
            pltpu.VMEM((n, per_dev, rank, width), bf16),
            pltpu.VMEM((n, rows_own, rank), bf16),
            pltpu.VMEM((n, rank, rows_own), bf16),
            dma, dma, dma((n,)), dma((n, chunks)), dma((n, chunks)), dma((n, chunks)),
            dma((reps,)), dma((reps,)), dma((reps,)), dma((reps,)),
            dma((n,)), dma((n,)), dma((n,)), dma((n,)),
        ],
        compiler_params=pltpu.CompilerParams(
            collective_id=0, has_side_effects=True, vmem_limit_bytes=44 * 1024 * 1024),
        cost_estimate=pl.CostEstimate(
            flops=2 * rows * model_width * cols, bytes_accessed=2 * model_width * cols,
            transcendentals=0),
    )(recv, live, tokens, q_weight, a_out, b_out)


def solution(mesh):
    return jax.shard_map(
        per_device,
        mesh=mesh,
        in_specs=(
            P(("parts", "rep", "tp"), None),
            P(None, "tp"),
            P(("parts", "rep"), "tp", None),
            P(("parts", "rep"), None, "tp"),
            P("parts"),
            P("parts", None),
            P("parts", None),
        ),
        out_specs=P(("parts", "rep"), "tp"),
        check_vma=False,
    )
```

```python
import functools

import jax
import jax.numpy as jnp
from jax import lax
from jax.experimental import pallas as pl
from jax.experimental.pallas import tpu as pltpu
from jax.sharding import PartitionSpec as P

MESH = pl.DeviceIdType.MESH


def kernel(
    n, reps, depth, block_rows,
    recv_ref, live_ref, tok_hbm, w_hbm, a_out, b_out, o_hbm,
    w, toks, obuf, acc, a_in, b_in, a_sel, a_own, low, low_t,
    w_sem, own_sem, out_sem, rsend, lsend, trecv,
    a_send, a_recv, b_send, b_recv, ta_send, ta_recv, low_send, low_recv,
):
    me = lax.axis_index("tp")
    rep = lax.axis_index("rep")
    rows_own = toks.shape[1]
    chunks = toks.shape[2] // depth
    cols = obuf.shape[1]
    blocks, rank, width = a_sel.shape
    per_dev = a_own.shape[1]
    cap = a_out.shape[1]
    tile = min(512, cols)

    barrier = pltpu.get_barrier_semaphore()
    for i in range(1, n):
        pl.semaphore_signal(
            barrier, inc=1, device_id={"tp": lax.rem(me + i, n)}, device_id_type=MESH)
    for i in range(1, reps):
        pl.semaphore_signal(
            barrier, inc=1, device_id={"rep": lax.rem(rep + i, reps)}, device_id_type=MESH)
    pl.semaphore_wait(barrier, n - 1 + reps - 1)

    def part_of(c):
        return pl.ds(pl.multiple_of(c * depth, depth), depth)

    def send(src, s, c, to, sems):
        return pltpu.make_async_remote_copy(
            src_ref=src, dst_ref=toks.at[s, :, part_of(c)],
            send_sem=sems.at[s, c], recv_sem=trecv.at[s, c],
            device_id={"tp": to}, device_id_type=MESH)

    def right_send(src, s, c):
        return send(src, s, c, jnp.minimum(me + 1, n - 1), rsend)

    def left_send(src, s, c):
        return send(src, s, c, jnp.maximum(me - 1, 0), lsend)

    def send_own(c):
        src = tok_hbm.at[:, part_of(c)]

        @pl.when(me < n - 1)
        def _():
            right_send(src, me, c).start()

        @pl.when(me > 0)
        def _():
            left_send(src, me, c).start()

    def rep_copy(src, dst, to, sends, recvs):
        return pltpu.make_async_remote_copy(
            src_ref=src.at[to], dst_ref=dst.at[rep],
            send_sem=sends.at[to], recv_sem=recvs.at[rep],
            device_id={"rep": to}, device_id_type=MESH)

    def rep_arrival(dst, frm, sends, recvs):
        return pltpu.make_async_remote_copy(
            src_ref=dst.at[frm], dst_ref=dst.at[frm],
            send_sem=sends.at[frm], recv_sem=recvs.at[frm],
            device_id={"rep": frm}, device_id_type=MESH)

    early = max(1, chunks // 2)
    for i in range(1, reps):
        rep_copy(a_out, a_in, lax.rem(rep + i, reps), a_send, a_recv).start()
    for c in range(early):
        send_own(c)
    own_a = pltpu.make_async_copy(a_out.at[rep], a_in.at[rep], a_recv.at[rep])
    own_b = pltpu.make_async_copy(b_out.at[rep], b_in.at[rep], b_recv.at[rep])
    own_a.start()
    for i in range(1, reps):
        rep_copy(b_out, b_in, lax.rem(rep + i, reps), b_send, b_recv).start()
    own_b.start()
    own_t = pltpu.make_async_copy(tok_hbm, toks.at[me], own_sem)
    own_t.start()
    w_copy = pltpu.make_async_copy(w_hbm, w, w_sem)
    w_copy.start()

    own_a.wait()
    for i in range(1, reps):
        rep_arrival(a_in, lax.rem(rep + i, reps), a_send, a_recv).wait_recv()
    for b in range(blocks):
        at = recv_ref[b]
        a_sel[b] = a_in[at // cap, at % cap]

    def first_block(d):
        return d * rows_own // block_rows

    def ta_copy(d):
        return pltpu.make_async_remote_copy(
            src_ref=a_sel.at[pl.ds(first_block(d), per_dev)], dst_ref=a_own.at[me],
            send_sem=ta_send.at[d], recv_sem=ta_recv.at[me],
            device_id={"tp": d}, device_id_type=MESH)

    def ta_arrival(d):
        return pltpu.make_async_remote_copy(
            src_ref=a_own.at[d], dst_ref=a_own.at[d],
            send_sem=ta_send.at[d], recv_sem=ta_recv.at[d],
            device_id={"tp": d}, device_id_type=MESH)

    for i in range(1, n):
        ta_copy(lax.rem(me + i, n)).start()
    for c in range(early, chunks):
        send_own(c)
    a_own[me] = a_sel[pl.ds(first_block(me), per_dev)]
    def forward(k, c):
        from_left = jnp.maximum(me - k, 0)
        from_right = jnp.minimum(me + k, n - 1)

        @pl.when(me - k >= 0)
        def _():
            here = toks.at[from_left, :, part_of(c)]
            right_send(here, from_left, c).wait_recv()

            @pl.when(me < n - 1)
            def _():
                right_send(here, from_left, c).start()

        @pl.when(me + k < n)
        def _():
            here = toks.at[from_right, :, part_of(c)]
            left_send(here, from_right, c).wait_recv()

            @pl.when(me > 0)
            def _():
                left_send(here, from_right, c).start()

    @pl.loop(0, chunks)
    def _(c):
        forward(1, c)

    own_t.wait()
    for i in range(1, n):
        ta_arrival(lax.rem(me + i, n)).wait_recv()

    part = rows_own // per_dev
    for j in range(per_dev):
        total = jnp.zeros((part, rank), jnp.float32)
        for k in range(n):
            total += lax.dot_general(
                toks[me, j * part:(j + 1) * part, k * width:(k + 1) * width], a_own[k, j],
                (((1,), (1,)), ((), ())), preferred_element_type=jnp.float32)
        low[me, j * part:(j + 1) * part, :] = total.astype(jnp.bfloat16)
        low_t[me, :, j * part:(j + 1) * part] = total.T.astype(jnp.bfloat16)

    def low_copy(d):
        return pltpu.make_async_remote_copy(
            src_ref=low_t.at[me], dst_ref=low_t.at[me],
            send_sem=low_send.at[d], recv_sem=low_recv.at[me],
            device_id={"tp": d}, device_id_type=MESH)

    def low_arrival(d):
        return pltpu.make_async_remote_copy(
            src_ref=low_t.at[d], dst_ref=low_t.at[d],
            send_sem=low_send.at[d], recv_sem=low_recv.at[d],
            device_id={"tp": d}, device_id_type=MESH)

    for i in range(1, n):
        low_copy(lax.rem(me + i, n)).start()

    own_b.wait()
    for i in range(1, reps):
        rep_arrival(b_in, lax.rem(rep + i, reps), b_send, b_recv).wait_recv()
    w_copy.wait()

    def out_rows(s):
        return pl.ds(pl.multiple_of(s * rows_own, rows_own), rows_own)

    def out_copy(s):
        return pltpu.make_async_copy(obuf.at[out_rows(s)], o_hbm.at[out_rows(s)], out_sem.at[s])

    def tiles(body):
        @pl.loop(0, cols // tile)
        def _(t):
            body(pl.ds(pl.multiple_of(t * tile, tile), tile))

    def adapter(s, side):
        for j in range(per_dev):
            first = s * rows_own + j * part
            block = first // block_rows
            at = recv_ref[block]
            at_row = lax.broadcasted_iota(jnp.int32, (part, tile), 0)
            valid = lax.rem(first, block_rows) + at_row < live_ref[block]

            def body(cs):
                extra = jnp.dot(
                    low[s, j * part:(j + 1) * part, :], b_in[at // cap, at % cap, :, cs],
                    preferred_element_type=jnp.float32)
                acc[side, j * part:(j + 1) * part, cs] = jnp.where(valid, extra, 0.0)

            tiles(body)

    def multiply(s, c, side):
        @pl.when(c == 0)
        def _():
            adapter(s, side)

        def product(cs):
            return acc[side, :, cs] + jnp.dot(
                toks[s, :, part_of(c)], w[part_of(c), cs], preferred_element_type=jnp.float32)

        @pl.when(c < chunks - 1)
        def _():
            def body(cs):
                acc[side, :, cs] = product(cs)

            tiles(body)

        @pl.when(c == chunks - 1)
        def _():
            def body(cs):
                obuf[out_rows(s), cs] = product(cs).astype(jnp.bfloat16)

            tiles(body)
            out_copy(s).start()

    def take_low(s):
        low_arrival(s).wait_recv()
        low[s] = low_t[s].astype(jnp.float32).T.astype(jnp.bfloat16)

    def take(side, k, c, slot):
        source = jnp.maximum(me - k, 0) if side == 0 else jnp.minimum(me + k, n - 1)

        @pl.when(me - k >= 0 if side == 0 else me + k < n)
        def _():
            @pl.when(c == 0)
            def _():
                take_low(source)

            multiply(source, c, slot)

    @pl.loop(chunks, (n - 1) * chunks)
    def _(e):
        k = e // chunks + 1
        c = lax.rem(e, chunks)
        take(0, k - 1, c, 0)
        take(1, k - 1, c, 1)

        @pl.when(k == 2)
        def _():
            multiply(me, c, 2)

        forward(k, c)

        @pl.when(k == n - 1)
        def _():
            take(0, k, c, 2)
            take(1, k, c, 2)

    for i in range(1, reps):
        to = lax.rem(rep + i, reps)
        rep_copy(a_out, a_in, to, a_send, a_recv).wait_send()
        rep_copy(b_out, b_in, to, b_send, b_recv).wait_send()
    for i in range(1, n):
        to = lax.rem(me + i, n)
        ta_copy(to).wait_send()
        low_copy(to).wait_send()

    @pl.loop(0, n)
    def _(s):
        out_copy(s).wait()

    @pl.loop(0, n * chunks)
    def _(e):
        s = e // chunks
        c = lax.rem(e, chunks)
        here = toks.at[s, :, part_of(c)]

        @pl.when((s <= me) & (me < n - 1))
        def _():
            right_send(here, s, c).wait_send()

        @pl.when((s >= me) & (me > 0))
        def _():
            left_send(here, s, c).wait_send()


def fetch(
    reps, cap,
    row_ref, adapter_ref, length_ref, a_hbm, b_hbm, a_out, b_out, recv_ref, live_ref,
    source, seen, a_sem, b_sem,
):
    rep = lax.axis_index("rep")
    slots = a_hbm.shape[0]
    blocks = adapter_ref.shape[1]
    for i in range(reps * cap):
        source[i] = 0
    for i in range(reps):
        seen[i] = 0

    @pl.loop(0, reps)
    def _(r):
        def block(b, held):
            stored = row_ref[adapter_ref[r, b]]
            mine = stored // slots == rep

            @pl.when(mine)
            def _():
                source[r * cap + jnp.minimum(held, cap - 1)] = stored % slots

            return held + mine.astype(jnp.int32)

        lax.fori_loop(0, blocks, block, jnp.int32(0))

    def copies(i):
        at = source[i]
        return (
            pltpu.make_async_copy(a_hbm.at[at], a_out.at[i], a_sem.at[i]),
            pltpu.make_async_copy(b_hbm.at[at], b_out.at[i], b_sem.at[i]),
        )

    for i in range(reps * cap):
        for copy in copies(i):
            copy.start()

    @pl.loop(0, blocks)
    def _(b):
        owner = row_ref[adapter_ref[rep, b]] // slots
        place = seen[owner]
        recv_ref[b] = owner * cap + place
        seen[owner] = place + 1
        live_ref[b] = length_ref[rep, b]

    for i in range(reps * cap):
        for copy in copies(i):
            copy.wait()


def per_device(tokens, q_weight, a_store, b_store, store_row, block_adapter, block_length):
    n = lax.axis_size("tp")
    reps = lax.axis_size("rep")
    here_rep = lax.axis_index("rep")
    slot_count, width, rank = a_store.shape
    cols = b_store.shape[2]
    rows_own, model_width = tokens.shape
    blocks = block_adapter.shape[1]
    cap = max(2, -(-blocks // reps))
    block_rows = rows_own * n // blocks
    depth = model_width // 5
    chunks = model_width // depth
    per_dev = max(1, rows_own // block_rows)

    any_spec = pl.BlockSpec(memory_space=pl.ANY)
    smem = pl.BlockSpec(memory_space=pltpu.SMEM)
    vmem = pl.BlockSpec(memory_space=pltpu.VMEM)
    dma = pltpu.SemaphoreType.DMA
    bf16 = jnp.bfloat16
    rows = rows_own * n
    a_t = jnp.transpose(a_store, (0, 2, 1))
    a_out, b_out, recv, live = pl.pallas_call(
        functools.partial(fetch, reps, cap),
        out_shape=(
            jax.ShapeDtypeStruct((reps * cap, rank, width), bf16),
            jax.ShapeDtypeStruct((reps * cap, rank, cols), bf16),
            jax.ShapeDtypeStruct((blocks,), jnp.int32),
            jax.ShapeDtypeStruct((blocks,), jnp.int32),
        ),
        in_specs=[smem, smem, smem, any_spec, any_spec],
        out_specs=(vmem, vmem, smem, smem),
        scratch_shapes=[
            pltpu.SMEM((reps * cap,), jnp.int32), pltpu.SMEM((reps,), jnp.int32),
            dma((reps * cap,)), dma((reps * cap,)),
        ],
    )(store_row, block_adapter, block_length, a_t, b_store)
    a_out = a_out.reshape(reps, cap, rank, width)
    b_out = b_out.reshape(reps, cap, rank, cols)
    return pl.pallas_call(
        functools.partial(kernel, n, reps, depth, block_rows),
        out_shape=jax.ShapeDtypeStruct((rows, cols), bf16),
        in_specs=[smem, smem, any_spec, any_spec, any_spec, any_spec],
        out_specs=any_spec,
        scratch_shapes=[
            pltpu.VMEM((model_width, cols), bf16),
            pltpu.VMEM((n, rows_own, model_width), bf16),
            pltpu.VMEM((rows, cols), bf16),
            pltpu.VMEM((3, rows_own, cols), jnp.float32),
            pltpu.VMEM((reps, cap, rank, width), bf16),
            pltpu.VMEM((reps, cap, rank, cols), bf16),
            pltpu.VMEM((blocks, rank, width), bf16),
            pltpu.VMEM((n, per_dev, rank, width), bf16),
            pltpu.VMEM((n, rows_own, rank), bf16),
            pltpu.VMEM((n, rank, rows_own), bf16),
            dma, dma, dma((n,)), dma((n, chunks)), dma((n, chunks)), dma((n, chunks)),
            dma((reps,)), dma((reps,)), dma((reps,)), dma((reps,)),
            dma((n,)), dma((n,)), dma((n,)), dma((n,)),
        ],
        compiler_params=pltpu.CompilerParams(
            collective_id=0, has_side_effects=True, vmem_limit_bytes=44 * 1024 * 1024),
        cost_estimate=pl.CostEstimate(
            flops=2 * rows * model_width * cols, bytes_accessed=2 * model_width * cols,
            transcendentals=0),
    )(recv, live, tokens, q_weight, a_out, b_out)


def solution(mesh):
    return jax.shard_map(
        per_device,
        mesh=mesh,
        in_specs=(
            P(("parts", "rep", "tp"), None),
            P(None, "tp"),
            P(("parts", "rep"), "tp", None),
            P(("parts", "rep"), None, "tp"),
            P("parts"),
            P("parts", None),
            P("parts", None),
        ),
        out_specs=P(("parts", "rep"), "tp"),
        check_vma=False,
    )
```

```python
import functools

import jax
import jax.numpy as jnp
from jax import lax
from jax.experimental import pallas as pl
from jax.experimental.pallas import tpu as pltpu
from jax.sharding import PartitionSpec as P

MESH = pl.DeviceIdType.MESH


def kernel(
    n, reps, depth, block_rows,
    recv_ref, live_ref, tok_hbm, w_hbm, a_out, b_out, o_hbm,
    w, toks, obuf, acc, a_in, b_in, a_sel, a_own, low, low_t,
    w_sem, own_sem, out_sem, rsend, lsend, trecv,
    a_send, a_recv, b_send, b_recv, ta_send, ta_recv, low_send, low_recv,
):
    me = lax.axis_index("tp")
    rep = lax.axis_index("rep")
    rows_own = toks.shape[1]
    chunks = toks.shape[2] // depth
    cols = obuf.shape[1]
    blocks, rank, width = a_sel.shape
    per_dev = a_own.shape[1]
    cap = a_out.shape[1]
    tile = min(512, cols)

    barrier = pltpu.get_barrier_semaphore()
    for i in range(1, n):
        pl.semaphore_signal(
            barrier, inc=1, device_id={"tp": lax.rem(me + i, n)}, device_id_type=MESH)
    for i in range(1, reps):
        pl.semaphore_signal(
            barrier, inc=1, device_id={"rep": lax.rem(rep + i, reps)}, device_id_type=MESH)
    pl.semaphore_wait(barrier, n - 1 + reps - 1)

    def part_of(c):
        return pl.ds(pl.multiple_of(c * depth, depth), depth)

    def send(src, s, c, to, sems):
        return pltpu.make_async_remote_copy(
            src_ref=src, dst_ref=toks.at[s, :, part_of(c)],
            send_sem=sems.at[s, c], recv_sem=trecv.at[s, c],
            device_id={"tp": to}, device_id_type=MESH)

    def right_send(src, s, c):
        return send(src, s, c, jnp.minimum(me + 1, n - 1), rsend)

    def left_send(src, s, c):
        return send(src, s, c, jnp.maximum(me - 1, 0), lsend)

    def send_own(c):
        src = tok_hbm.at[:, part_of(c)]

        @pl.when(me < n - 1)
        def _():
            right_send(src, me, c).start()

        @pl.when(me > 0)
        def _():
            left_send(src, me, c).start()

    def rep_copy(src, dst, to, sends, recvs):
        return pltpu.make_async_remote_copy(
            src_ref=src.at[to], dst_ref=dst.at[rep],
            send_sem=sends.at[to], recv_sem=recvs.at[rep],
            device_id={"rep": to}, device_id_type=MESH)

    def rep_arrival(dst, frm, sends, recvs):
        return pltpu.make_async_remote_copy(
            src_ref=dst.at[frm], dst_ref=dst.at[frm],
            send_sem=sends.at[frm], recv_sem=recvs.at[frm],
            device_id={"rep": frm}, device_id_type=MESH)

    early = max(1, chunks // 2)
    for i in range(1, reps):
        rep_copy(a_out, a_in, lax.rem(rep + i, reps), a_send, a_recv).start()
    for c in range(early):
        send_own(c)
    own_a = pltpu.make_async_copy(a_out.at[rep], a_in.at[rep], a_recv.at[rep])
    own_b = pltpu.make_async_copy(b_out.at[rep], b_in.at[rep], b_recv.at[rep])
    own_a.start()
    for i in range(1, reps):
        rep_copy(b_out, b_in, lax.rem(rep + i, reps), b_send, b_recv).start()
    own_b.start()
    own_t = pltpu.make_async_copy(tok_hbm, toks.at[me], own_sem)
    own_t.start()
    w_copy = pltpu.make_async_copy(w_hbm, w, w_sem)
    w_copy.start()

    own_a.wait()
    for i in range(1, reps):
        rep_arrival(a_in, lax.rem(rep + i, reps), a_send, a_recv).wait_recv()
    for b in range(blocks):
        at = recv_ref[b]
        a_sel[b] = a_in[at // cap, at % cap]

    def first_block(d):
        return d * rows_own // block_rows

    def ta_copy(d):
        return pltpu.make_async_remote_copy(
            src_ref=a_sel.at[pl.ds(first_block(d), per_dev)], dst_ref=a_own.at[me],
            send_sem=ta_send.at[d], recv_sem=ta_recv.at[me],
            device_id={"tp": d}, device_id_type=MESH)

    def ta_arrival(d):
        return pltpu.make_async_remote_copy(
            src_ref=a_own.at[d], dst_ref=a_own.at[d],
            send_sem=ta_send.at[d], recv_sem=ta_recv.at[d],
            device_id={"tp": d}, device_id_type=MESH)

    for i in range(1, n):
        ta_copy(lax.rem(me + i, n)).start()
    for c in range(early, chunks):
        send_own(c)
    a_own[me] = a_sel[pl.ds(first_block(me), per_dev)]
    def forward(k, c):
        from_left = jnp.maximum(me - k, 0)
        from_right = jnp.minimum(me + k, n - 1)

        @pl.when(me - k >= 0)
        def _():
            here = toks.at[from_left, :, part_of(c)]
            right_send(here, from_left, c).wait_recv()

            @pl.when(me < n - 1)
            def _():
                right_send(here, from_left, c).start()

        @pl.when(me + k < n)
        def _():
            here = toks.at[from_right, :, part_of(c)]
            left_send(here, from_right, c).wait_recv()

            @pl.when(me > 0)
            def _():
                left_send(here, from_right, c).start()

    @pl.loop(0, chunks)
    def _(c):
        forward(1, c)

    own_t.wait()
    for i in range(1, n):
        ta_arrival(lax.rem(me + i, n)).wait_recv()

    part = rows_own // per_dev
    for j in range(per_dev):
        total = jnp.zeros((part, rank), jnp.float32)
        for k in range(n):
            total += lax.dot_general(
                toks[me, j * part:(j + 1) * part, k * width:(k + 1) * width], a_own[k, j],
                (((1,), (1,)), ((), ())), preferred_element_type=jnp.float32)
        low[me, j * part:(j + 1) * part, :] = total.astype(jnp.bfloat16)
        low_t[me, :, j * part:(j + 1) * part] = total.T.astype(jnp.bfloat16)

    def low_copy(d):
        return pltpu.make_async_remote_copy(
            src_ref=low_t.at[me], dst_ref=low_t.at[me],
            send_sem=low_send.at[d], recv_sem=low_recv.at[me],
            device_id={"tp": d}, device_id_type=MESH)

    def low_arrival(d):
        return pltpu.make_async_remote_copy(
            src_ref=low_t.at[d], dst_ref=low_t.at[d],
            send_sem=low_send.at[d], recv_sem=low_recv.at[d],
            device_id={"tp": d}, device_id_type=MESH)

    for i in range(1, n):
        low_copy(lax.rem(me + i, n)).start()

    own_b.wait()
    for i in range(1, reps):
        rep_arrival(b_in, lax.rem(rep + i, reps), b_send, b_recv).wait_recv()
    w_copy.wait()

    def out_rows(s):
        return pl.ds(pl.multiple_of(s * rows_own, rows_own), rows_own)

    def out_copy(s):
        return pltpu.make_async_copy(obuf.at[out_rows(s)], o_hbm.at[out_rows(s)], out_sem.at[s])

    def tiles(body):
        @pl.loop(0, cols // tile)
        def _(t):
            body(pl.ds(pl.multiple_of(t * tile, tile), tile))

    def adapter(s, side):
        for j in range(per_dev):
            first = s * rows_own + j * part
            block = first // block_rows
            at = recv_ref[block]
            at_row = lax.broadcasted_iota(jnp.int32, (part, tile), 0)
            valid = lax.rem(first, block_rows) + at_row < live_ref[block]

            def body(cs):
                extra = jnp.dot(
                    low[s, j * part:(j + 1) * part, :], b_in[at // cap, at % cap, :, cs],
                    preferred_element_type=jnp.float32)
                acc[side, j * part:(j + 1) * part, cs] = jnp.where(valid, extra, 0.0)

            tiles(body)

    def multiply(s, c, side):
        @pl.when(c == 0)
        def _():
            adapter(s, side)

        def product(cs):
            return acc[side, :, cs] + jnp.dot(
                toks[s, :, part_of(c)], w[part_of(c), cs], preferred_element_type=jnp.float32)

        @pl.when(c < chunks - 1)
        def _():
            def body(cs):
                acc[side, :, cs] = product(cs)

            tiles(body)

        @pl.when(c == chunks - 1)
        def _():
            def body(cs):
                obuf[out_rows(s), cs] = product(cs).astype(jnp.bfloat16)

            tiles(body)
            out_copy(s).start()

    def take_low(s):
        low_arrival(s).wait_recv()
        low[s] = low_t[s].astype(jnp.float32).T.astype(jnp.bfloat16)

    def take(side, k, c, slot):
        source = jnp.maximum(me - k, 0) if side == 0 else jnp.minimum(me + k, n - 1)

        @pl.when(me - k >= 0 if side == 0 else me + k < n)
        def _():
            @pl.when(c == 0)
            def _():
                take_low(source)

            multiply(source, c, slot)

    @pl.loop(chunks, (n - 1) * chunks)
    def _(e):
        k = e // chunks + 1
        c = lax.rem(e, chunks)
        @pl.when(k < n - 1)
        def _():
            forward(k, c)

        take(0, k - 1, c, 0)
        take(1, k - 1, c, 1)

        @pl.when(k == 2)
        def _():
            multiply(me, c, 2)

        @pl.when(k == n - 1)
        def _():
            forward(k, c)
            take(0, k, c, 2)
            take(1, k, c, 2)

    for i in range(1, reps):
        to = lax.rem(rep + i, reps)
        rep_copy(a_out, a_in, to, a_send, a_recv).wait_send()
        rep_copy(b_out, b_in, to, b_send, b_recv).wait_send()
    for i in range(1, n):
        to = lax.rem(me + i, n)
        ta_copy(to).wait_send()
        low_copy(to).wait_send()

    @pl.loop(0, n)
    def _(s):
        out_copy(s).wait()

    @pl.loop(0, n * chunks)
    def _(e):
        s = e // chunks
        c = lax.rem(e, chunks)
        here = toks.at[s, :, part_of(c)]

        @pl.when((s <= me) & (me < n - 1))
        def _():
            right_send(here, s, c).wait_send()

        @pl.when((s >= me) & (me > 0))
        def _():
            left_send(here, s, c).wait_send()


def fetch(
    reps, cap,
    row_ref, adapter_ref, length_ref, a_hbm, b_hbm, a_out, b_out, recv_ref, live_ref,
    source, seen, a_sem, b_sem,
):
    rep = lax.axis_index("rep")
    slots = a_hbm.shape[0]
    blocks = adapter_ref.shape[1]
    for i in range(reps * cap):
        source[i] = 0
    for i in range(reps):
        seen[i] = 0

    @pl.loop(0, reps)
    def _(r):
        def block(b, held):
            stored = row_ref[adapter_ref[r, b]]
            mine = stored // slots == rep

            @pl.when(mine)
            def _():
                source[r * cap + jnp.minimum(held, cap - 1)] = stored % slots

            return held + mine.astype(jnp.int32)

        lax.fori_loop(0, blocks, block, jnp.int32(0))

    def copies(i):
        at = source[i]
        return (
            pltpu.make_async_copy(a_hbm.at[at], a_out.at[i], a_sem.at[i]),
            pltpu.make_async_copy(b_hbm.at[at], b_out.at[i], b_sem.at[i]),
        )

    for i in range(reps * cap):
        for copy in copies(i):
            copy.start()

    @pl.loop(0, blocks)
    def _(b):
        owner = row_ref[adapter_ref[rep, b]] // slots
        place = seen[owner]
        recv_ref[b] = owner * cap + place
        seen[owner] = place + 1
        live_ref[b] = length_ref[rep, b]

    for i in range(reps * cap):
        for copy in copies(i):
            copy.wait()


def per_device(tokens, q_weight, a_store, b_store, store_row, block_adapter, block_length):
    n = lax.axis_size("tp")
    reps = lax.axis_size("rep")
    here_rep = lax.axis_index("rep")
    slot_count, width, rank = a_store.shape
    cols = b_store.shape[2]
    rows_own, model_width = tokens.shape
    blocks = block_adapter.shape[1]
    cap = max(2, -(-blocks // reps))
    block_rows = rows_own * n // blocks
    depth = model_width // 5
    chunks = model_width // depth
    per_dev = max(1, rows_own // block_rows)

    any_spec = pl.BlockSpec(memory_space=pl.ANY)
    smem = pl.BlockSpec(memory_space=pltpu.SMEM)
    vmem = pl.BlockSpec(memory_space=pltpu.VMEM)
    dma = pltpu.SemaphoreType.DMA
    bf16 = jnp.bfloat16
    rows = rows_own * n
    a_t = jnp.transpose(a_store, (0, 2, 1))
    a_out, b_out, recv, live = pl.pallas_call(
        functools.partial(fetch, reps, cap),
        out_shape=(
            jax.ShapeDtypeStruct((reps * cap, rank, width), bf16),
            jax.ShapeDtypeStruct((reps * cap, rank, cols), bf16),
            jax.ShapeDtypeStruct((blocks,), jnp.int32),
            jax.ShapeDtypeStruct((blocks,), jnp.int32),
        ),
        in_specs=[smem, smem, smem, any_spec, any_spec],
        out_specs=(vmem, vmem, smem, smem),
        scratch_shapes=[
            pltpu.SMEM((reps * cap,), jnp.int32), pltpu.SMEM((reps,), jnp.int32),
            dma((reps * cap,)), dma((reps * cap,)),
        ],
    )(store_row, block_adapter, block_length, a_t, b_store)
    a_out = a_out.reshape(reps, cap, rank, width)
    b_out = b_out.reshape(reps, cap, rank, cols)
    return pl.pallas_call(
        functools.partial(kernel, n, reps, depth, block_rows),
        out_shape=jax.ShapeDtypeStruct((rows, cols), bf16),
        in_specs=[smem, smem, any_spec, any_spec, any_spec, any_spec],
        out_specs=any_spec,
        scratch_shapes=[
            pltpu.VMEM((model_width, cols), bf16),
            pltpu.VMEM((n, rows_own, model_width), bf16),
            pltpu.VMEM((rows, cols), bf16),
            pltpu.VMEM((3, rows_own, cols), jnp.float32),
            pltpu.VMEM((reps, cap, rank, width), bf16),
            pltpu.VMEM((reps, cap, rank, cols), bf16),
            pltpu.VMEM((blocks, rank, width), bf16),
            pltpu.VMEM((n, per_dev, rank, width), bf16),
            pltpu.VMEM((n, rows_own, rank), bf16),
            pltpu.VMEM((n, rank, rows_own), bf16),
            dma, dma, dma((n,)), dma((n, chunks)), dma((n, chunks)), dma((n, chunks)),
            dma((reps,)), dma((reps,)), dma((reps,)), dma((reps,)),
            dma((n,)), dma((n,)), dma((n,)), dma((n,)),
        ],
        compiler_params=pltpu.CompilerParams(
            collective_id=0, has_side_effects=True, vmem_limit_bytes=44 * 1024 * 1024),
        cost_estimate=pl.CostEstimate(
            flops=2 * rows * model_width * cols, bytes_accessed=2 * model_width * cols,
            transcendentals=0),
    )(recv, live, tokens, q_weight, a_out, b_out)


def solution(mesh):
    return jax.shard_map(
        per_device,
        mesh=mesh,
        in_specs=(
            P(("parts", "rep", "tp"), None),
            P(None, "tp"),
            P(("parts", "rep"), "tp", None),
            P(("parts", "rep"), None, "tp"),
            P("parts"),
            P("parts", None),
            P("parts", None),
        ),
        out_specs=P(("parts", "rep"), "tp"),
        check_vma=False,
    )
```
